256 devices in a mesh: freq: 16 (over z, core), tcol: 16 (over x, y).
Axes of the slice: x: 4, y: 4, z: 8, core: 2. Of those that a mesh axis runs over, the one named last changes fastest.
Arguments:
- kernel_v: bfloat16 [16, 32, 64, 2, 32, 256], P('freq', None, 'tcol'), may hold values from -0.25 to 0.25
- kernel_u: bfloat16 [16, 32, 64, 2, 32, 256], P('freq', 'tcol'), may hold values from -0.125 to 0.125
- sources: bfloat16 [16, 2, 16384, 256], P('freq', None, 'tcol'), may hold values from -6 to 6
- ranks: int32 [16, 32, 64], P('freq', None, 'tcol'), may hold values from 4 to 32, as said below
- row_owner: int32 [32], replicated, may hold values from 0 to 15, as said below
Outputs:
- seismo: float32 [16, 32, 256, 256], P('freq', 'tcol')
The draws below stay inside these ranges and needn't reach their ends.
Inputs may be any that keep to these rules, and one draw needn't show every extreme that they name: Ranks are whole numbers; the bounds are reached for every frequency. For every frequency, owner o and index d of tcol, the ranks of the tiles in tile rows owned by o and tile columns d * 4 to (d + 1) * 4 - 1 sum to at most 192, and this total is reached for every frequency. `row_owner`: every index of tcol owns exactly 2 tile rows.
All inputs are finite; a program needn't handle non-finite values.
Results may differ from the reference program's by a relative error of at most 0.0029.
Values may be sent and summed in bfloat16 or wider, within the bound.
A program may use at most 64 MiB of HBM per device.

```python
import jax
import jax.numpy as jnp
from jax import lax

TS = 256
RMAX = 32
S = 256
TC_DEV = 4
OWN = 2
TCOLS = 64
TROWS = 32
NCOLS = 16384
NF = 16
NT = 16


def owner_table(key):
    shared = jax.random.fold_in(key, 5)
    owners = (jax.random.permutation(shared, TROWS) // OWN).astype(jnp.int32)
    keys = owners * TROWS + jnp.arange(TROWS, dtype=jnp.int32)
    order = jnp.argsort(keys).astype(jnp.int32)
    return (owners, order)


def draw_ranks(key, part):
    owners, order = owner_table(key)
    key = jax.random.fold_in(key, 11)
    first_key, second_key = jax.random.split(key)
    lowest = max(1, RMAX // 8)
    pairs = TROWS // 2
    first = jax.random.randint(first_key, (NF, pairs, TCOLS), lowest, RMAX + 1)
    first = first.at[:, :OWN // 2, :TC_DEV].set(RMAX)
    first = first.at[:, OWN // 2, 0].set(lowest)
    upper = jnp.minimum(RMAX, 3 * RMAX // 2 - first) + 1
    second = jax.random.randint(second_key, (NF, pairs, TCOLS), lowest, upper)
    second = second.at[:, :OWN // 2, :TC_DEV].set(RMAX // 2)
    slotted = jnp.stack([first, second], axis=2).reshape(NF, TROWS, TCOLS)
    ranks = jnp.zeros((NF, TROWS, TCOLS), jnp.int32).at[:, order, :].set(slotted.astype(jnp.int32))
    return ranks.astype(jnp.int32)


def draw_row_owner(key, part):
    owners, order = owner_table(key)
    return owners.astype(jnp.int32)


def shard_levels(rng, extent, cuts, smallest, largest):
    def one(dim, shards_of):
        heights = jax.random.uniform(jax.random.fold_in(jax.random.fold_in(rng, 6), dim), (shards_of,), jnp.float32, smallest / len(cuts), largest / len(cuts))
        return jnp.repeat(jnp.exp(heights), extent[dim] // shards_of).reshape((-1,) + (1,) * (len(extent) - dim - 1))

    gain = one(*cuts[0])
    for cut in cuts[1:]:
        gain = gain * one(*cut)
    return gain


def normal_values(stream_key, extent, scale, bound, cuts=(), held_as=jnp.bfloat16):
    drawn = scale * jax.random.normal(stream_key, extent, jnp.float32)
    if cuts:
        drawn = drawn * shard_levels(stream_key, extent, cuts, -0.22, 0.18)
    return jnp.clip(drawn, -bound, bound).astype(held_as)


def setup_inputs(seed: int = 0) -> dict:
    arg_keys = jax.random.split(jax.random.key(seed), 6)
    return {
        "kernel_v": normal_values(arg_keys[0], (NF, TROWS, TCOLS, 2, RMAX, TS), (2 * TS) ** -0.5, 0.25, ((0, 16), (2, 16))),
        "kernel_u": normal_values(arg_keys[1], (NF, TROWS, TCOLS, 2, RMAX, TS), (TCOLS * RMAX) ** -0.5, 0.125, ((0, 16), (1, 16))),
        "sources": normal_values(arg_keys[2], (NF, 2, NCOLS, S), 1.0, 6.0, ((0, 16), (2, 16))),
        "ranks": draw_ranks(jax.random.fold_in(arg_keys[5], 71), 0),
        "row_owner": draw_row_owner(jax.random.fold_in(arg_keys[5], 71), 0),
    }


def owner_order(row_owner):
    count = row_owner.shape[0]
    keys = row_owner.astype(jnp.int32) * count + jnp.arange(count, dtype=jnp.int32)
    return jnp.argsort(keys).astype(jnp.int32)


def one_frequency(kernel_v, kernel_u, sources, ranks, order):
    tile = kernel_v.shape[-1]
    slots = kernel_v.shape[3]
    fields = sources.reshape(2, -1, tile, sources.shape[-1])
    prod = jnp.einsum('ijarc,bjcs->ijabrs', kernel_v.astype(jnp.float32), fields.astype(jnp.float32))
    coeff_real = prod[:, :, 0, 0] + prod[:, :, 1, 1]
    coeff_imag = prod[:, :, 0, 1] - prod[:, :, 1, 0]
    keep = (jnp.arange(slots, dtype=jnp.int32)[None, None, :] < ranks[:, :, None]).astype(jnp.float32)
    coeff = (jnp.stack([coeff_real, coeff_imag], axis=2) * keep[:, :, None, :, None]).astype(jnp.bfloat16)
    moved = jnp.take(coeff, order, axis=0)
    quad = jnp.einsum('qjart,qjbrs->qabts', kernel_u.astype(jnp.float32), moved.astype(jnp.float32))
    return quad[:, 0, 0] - quad[:, 1, 1], quad[:, 0, 1] + quad[:, 1, 0]


def reference(kernel_v, kernel_u, sources, ranks, row_owner):
    order = owner_order(row_owner)

    def per_freq(items):
        return one_frequency(items[0], items[1], items[2], items[3], order)

    y_real, y_imag = lax.map(per_freq, (kernel_v, kernel_u, sources, ranks))
    times = jnp.arange(NT, dtype=jnp.int32)
    freqs = jnp.arange(NF, dtype=jnp.int32)
    phase = ((freqs[None, :] + 1) * times[:, None]) % (2 * NT)
    angle = jnp.pi * phase.astype(jnp.float32) / NT
    scale = NF ** -0.5
    cos_tab = jnp.cos(angle) * scale
    sin_tab = jnp.sin(angle) * scale
    first = jnp.einsum('tk,kqas->tqas', cos_tab, y_real, precision=lax.Precision.HIGHEST)
    second = jnp.einsum('tk,kqas->tqas', sin_tab, y_imag, precision=lax.Precision.HIGHEST)
    return first - second
```

```python
import jax
import jax.numpy as jnp
from jax import lax
from jax.experimental import pallas as pl
from jax.experimental.pallas import tpu as pltpu
from jax.sharding import PartitionSpec as P

MESH = pl.DeviceIdType.MESH
NX, NY, NZ = 4, 4, 8
GROUPS = NX * NY
ROWS, COLS, SLOTS, TILE, WIDTH = 32, 4, 32, 256, 256
OWN = ROWS // GROUPS
PACK = 192
CHUNKS = 4
HALF = WIDTH // CHUNKS
LANES = 2 * HALF
DEPTH = GROUPS * PACK
LONG, SHORT = 4, 3

OFFSETS = (
    (2, 2), (2, 1), (1, 2), (2, 3), (3, 2), (1, 1), (3, 3), (1, 3), (3, 1),
    (2, 0), (0, 2), (1, 0), (3, 0), (0, 1), (0, 3),
)
PEERS = len(OFFSETS)


def swap_halves(v):
    return pltpu.roll(v, HALF, 1)


def kernel(
    order, table, v_hbm, u_hbm, x_hbm, tgt, out,
    v, u, x, xs, coeff, packed, arrived, heads, left, acc,
    mine, theirs, long_out, long_in, short_out, short_in,
    load_sem, head_send, head_recv, tile_send, tile_recv, pair_send, pair_recv,
    long_send, long_recv, short_send, short_recv,
):
    freq, here = lax.axis_index("freq"), lax.axis_index("tcol")
    z, core = freq // 2, freq % 2
    px, py = here // NY, here % NY

    loads = [
        pltpu.make_async_copy(x_hbm.at[0], x, load_sem.at[0]),
        pltpu.make_async_copy(v_hbm.at[0], v, load_sem.at[1]),
        pltpu.make_async_copy(u_hbm.at[0], u, load_sem.at[2]),
    ]
    for load in loads:
        load.start()

    def peer(k):
        dx, dy = OFFSETS[k]
        return ((px + dx) % NX) * NY + (py + dy) % NY

    sibling = (2 * z + 1 - core, here)
    sigma = 1 - 2 * core
    ahead = (2 * ((z + sigma + NZ) % NZ) + core, here)
    behind = (2 * ((z - sigma + NZ) % NZ) + core, here)

    barrier = pltpu.get_barrier_semaphore()
    partners = [(freq, peer(k)) for k in range(PEERS)] + [sibling, ahead, behind]
    for partner in partners:
        pl.semaphore_signal(barrier, inc=1, device_id=partner, device_id_type=MESH)
    pl.semaphore_wait(barrier, len(partners))

    def remote(src, dst, send, recv, device):
        return pltpu.make_async_remote_copy(
            src_ref=src, dst_ref=dst, send_sem=send, recv_sem=recv,
            device_id=device, device_id_type=MESH,
        )

    head_rows = pl.ds(pl.multiple_of(8 * here, 8), 8)
    head_copies = [
        remote(tgt.at[peer(k)], heads.at[head_rows], head_send.at[k], head_recv.at[k], (freq, peer(k)))
        for k in range(PEERS)
    ]
    for copy in head_copies:
        copy.start()
    heads[head_rows] = tgt[here]

    my_rows = pl.ds(pl.multiple_of(PACK * here, PACK), PACK)

    def tile_copy(c, k):
        return remote(
            packed.at[c, k], arrived.at[c, my_rows], tile_send.at[c, k], tile_recv.at[c, k], (freq, peer(k))
        )

    loads[0].wait()
    first = lax.broadcasted_iota(jnp.int32, (TILE, LANES), 1) < HALF
    rank_row = lax.broadcasted_iota(jnp.int32, (PACK, COLS * SLOTS), 0).astype(jnp.float32)
    for half in range(CHUNKS // 2):
        lanes = pl.ds(half * LANES, LANES)

        @pl.loop(0, COLS)
        def _(j):
            rows = pl.ds(pl.multiple_of(j * TILE, TILE), TILE)
            re = x[0, rows, lanes].astype(jnp.float32)
            im = x[1, rows, lanes].astype(jnp.float32)
            re_swap, im_swap = swap_halves(re), swap_halves(im)
            xs[j, 0, :, :LANES] = jnp.where(first, re, im_swap).astype(jnp.bfloat16)
            xs[j, 0, :, LANES:] = jnp.where(first, re_swap, im).astype(jnp.bfloat16)
            xs[j, 1, :, :LANES] = jnp.where(first, im, -re_swap).astype(jnp.bfloat16)
            xs[j, 1, :, LANES:] = jnp.where(first, im_swap, -re).astype(jnp.bfloat16)

        if half == 0:
            loads[1].wait()

        @pl.loop(0, COLS)
        def _(j):
            slot_rows = pl.ds(pl.multiple_of(j * SLOTS, SLOTS), SLOTS)
            for part in range(2):
                rows = pl.ds(part * (ROWS // 2), ROWS // 2)
                re = v[rows, j, 0].reshape(ROWS // 2 * SLOTS, TILE)
                im = v[rows, j, 1].reshape(ROWS // 2 * SLOTS, TILE)
                prod = jnp.dot(re, xs[j, 0], preferred_element_type=jnp.float32)
                prod += jnp.dot(im, xs[j, 1], preferred_element_type=jnp.float32)
                coeff[rows, slot_rows, :] = prod.astype(jnp.bfloat16).reshape(ROWS // 2, SLOTS, 2 * LANES)

        def pack(owner):
            total = None
            for q in range(OWN):
                pick = jnp.where(rank_row == tgt[owner, q : q + 1, :], 1.0, 0.0).astype(jnp.bfloat16)
                part = jnp.dot(pick, coeff[order[OWN * owner + q]], preferred_element_type=jnp.float32)
                total = part if total is None else total + part
            return total.astype(jnp.bfloat16)

        for k in range(PEERS):
            block = pack(peer(k))
            packed[2 * half, k] = block[:, :LANES]
            packed[2 * half + 1, k] = block[:, LANES:]
            tile_copy(2 * half, k).start()
        for k in range(PEERS):
            tile_copy(2 * half + 1, k).start()
        block = pack(here)
        arrived[2 * half, my_rows] = block[:, :LANES]
        arrived[2 * half + 1, my_rows] = block[:, LANES:]

    for copy in head_copies:
        copy.wait_recv()
    loads[2].wait()
    columns = jnp.transpose(heads[...])
    pair_row = lax.broadcasted_iota(jnp.int32, (COLS * SLOTS, 2 * PACK), 1).astype(jnp.float32)
    for e in range(GROUPS // 2):
        for q in range(OWN):
            sides = []
            for side in range(2):
                at = 8 * (2 * e + side) + q
                column = columns[:, at : at + 1] + float(side * PACK)
                sides.append(jnp.where(pair_row == column, 1.0, 0.0).astype(jnp.bfloat16))
            pick = jnp.concatenate(sides, axis=0)
            for a in range(2):
                block = u[q, 2 * COLS * e : 2 * COLS * (e + 1), a].reshape(2 * COLS * SLOTS, TILE)
                turned = lax.dot_general(block, pick, (((0,), (0,)), ((), ())), preferred_element_type=jnp.float32)
                at = (2 * q + a) * TILE
                left[at : at + TILE, 2 * PACK * e : 2 * PACK * (e + 1)] = turned.astype(jnp.bfloat16)

    for c in range(CHUNKS):
        for k in range(PEERS):
            tile_copy(c, k).wait_recv()
        fields = []
        for q in range(OWN):
            rows = pl.ds(2 * q * TILE, 2 * TILE)
            acc[...] = jnp.dot(left[rows, :], arrived[c], preferred_element_type=jnp.float32)
            turned = swap_halves(acc[TILE:])
            fields.append(acc[:TILE] + jnp.where(first, -turned, turned))
        mine[c, 0] = jnp.where(first, fields[0], swap_halves(fields[1]))
        mine[c, 1] = jnp.where(first, swap_halves(fields[0]), fields[1])
        pair = remote(mine.at[c], theirs.at[c], pair_send.at[c], pair_recv.at[c], sibling)
        pair.start()
        pair.wait_recv()

        def share(steps):
            dest = (z + sigma * steps + NZ) % NZ
            at = (2 * dest + core) * (2 * NZ)
            own, other = at + freq, at + 2 * z + 1 - core
            shift = 4 * NZ * NZ
            return (
                table[own] * mine[c, 0] - table[own + shift] * mine[c, 1]
                + table[other] * theirs[c, 0] - table[other + shift] * theirs[c, 1]
            )

        def long_copy(h):
            return remote(long_out.at[c, h], long_in.at[c, h], long_send.at[c, h], long_recv.at[c, h], ahead)

        def short_copy(h):
            return remote(short_out.at[c, h], short_in.at[c, h], short_send.at[c, h], short_recv.at[c, h], behind)

        for h in range(LONG):
            total = share(LONG - h)
            if h:
                long_copy(h - 1).wait_recv()
                total += long_in[c, h - 1].astype(jnp.float32)
            long_out[c, h] = total.astype(jnp.bfloat16)
            long_copy(h).start()
            if h < SHORT:
                total = share(h - SHORT)
                if h:
                    short_copy(h - 1).wait_recv()
                    total += short_in[c, h - 1].astype(jnp.float32)
                short_out[c, h] = total.astype(jnp.bfloat16)
                short_copy(h).start()
        total = share(0)
        short_copy(SHORT - 1).wait_recv()
        total += short_in[c, SHORT - 1].astype(jnp.float32)
        long_copy(LONG - 1).wait_recv()
        total += long_in[c, LONG - 1].astype(jnp.float32)
        turned = swap_halves(total)
        at = c * HALF
        if c % 2 == 0:
            out[0, 0, :, at : at + HALF] = total[:, :HALF]
            out[0, 1, :, at : at + HALF] = turned[:, :HALF]
        else:
            out[0, 0, :, at : at + HALF] = turned[:, HALF:]
            out[0, 1, :, at : at + HALF] = total[:, HALF:]

        pair.wait_send()
        for h in range(LONG):
            long_copy(h).wait_send()
        for h in range(SHORT):
            short_copy(h).wait_send()
        for k in range(PEERS):
            tile_copy(c, k).wait_send()
    for copy in head_copies:
        copy.wait_send()


def on_device(kernel_v, kernel_u, sources, ranks, row_owner):
    rows = jnp.arange(ROWS, dtype=jnp.int32)
    keys = row_owner * ROWS + rows
    slot = jnp.sum((keys[None, :] < keys[:, None]).astype(jnp.int32), axis=1)
    placed = slot[None, :] == rows[:, None]
    order = jnp.sum(jnp.where(placed, rows[None, :], 0), axis=1)
    slotted = jnp.sum(jnp.where(placed[:, :, None], ranks[0][None], 0), axis=1)
    slotted = slotted.reshape(GROUPS, OWN * COLS)
    tiles = jnp.arange(OWN * COLS, dtype=jnp.int32)
    start = jnp.sum(jnp.where(tiles[None, None, :] < tiles[None, :, None], slotted[:, None, :], 0), axis=2)
    slots = jnp.arange(SLOTS, dtype=jnp.int32)
    target = jnp.where(slots < slotted[:, :, None], start[:, :, None] + slots, -1000)
    target = target.astype(jnp.float32).reshape(GROUPS, OWN, COLS * SLOTS)
    target = jnp.pad(target, ((0, 0), (0, 8 - OWN), (0, 0)), constant_values=-1000.0)

    count = 2 * NZ
    index = jnp.arange(count, dtype=jnp.int32)
    phase = ((index[None, :] + 1) * index[:, None]) % (2 * count)
    angle = jnp.pi * phase.astype(jnp.float32) / count
    scale = count ** (-0.5)
    table = jnp.concatenate([(jnp.cos(angle) * scale).reshape(-1), (jnp.sin(angle) * scale).reshape(-1)])

    bf16, f32 = jnp.bfloat16, jnp.float32
    vmem, dma = pltpu.VMEM, pltpu.SemaphoreType.DMA
    whole = pl.BlockSpec(memory_space=pltpu.VMEM)
    scalars = pl.BlockSpec(memory_space=pltpu.SMEM)
    away = pl.BlockSpec(memory_space=pl.ANY)
    return pl.pallas_call(
        kernel,
        out_shape=jax.ShapeDtypeStruct((1, OWN, TILE, WIDTH), f32),
        in_specs=[scalars, scalars, away, away, away, whole],
        out_specs=whole,
        scratch_shapes=[
            vmem(kernel_v.shape[1:], bf16),
            vmem(kernel_u.shape[1:], bf16),
            vmem(sources.shape[1:], bf16),
            vmem((COLS, 2, TILE, 2 * LANES), bf16),
            vmem((ROWS, COLS * SLOTS, 2 * LANES), bf16),
            vmem((CHUNKS, PEERS, PACK, LANES), bf16),
            vmem((CHUNKS, DEPTH, LANES), bf16),
            vmem((8 * GROUPS, COLS * SLOTS), f32),
            vmem((2 * OWN * TILE, DEPTH), bf16),
            vmem((2 * TILE, LANES), f32),
            vmem((CHUNKS, 2, TILE, LANES), f32),
            vmem((CHUNKS, 2, TILE, LANES), f32),
            vmem((CHUNKS, LONG, TILE, LANES), bf16),
            vmem((CHUNKS, LONG, TILE, LANES), bf16),
            vmem((CHUNKS, SHORT, TILE, LANES), bf16),
            vmem((CHUNKS, SHORT, TILE, LANES), bf16),
            dma((3,)),
            dma((PEERS,)),
            dma((PEERS,)),
            dma((CHUNKS, PEERS)),
            dma((CHUNKS, PEERS)),
            dma((CHUNKS,)),
            dma((CHUNKS,)),
            dma((CHUNKS, LONG)),
            dma((CHUNKS, LONG)),
            dma((CHUNKS, SHORT)),
            dma((CHUNKS, SHORT)),
        ],
        compiler_params=pltpu.CompilerParams(
            collective_id=0, has_side_effects=True, vmem_limit_bytes=56 * 1024 * 1024
        ),
        cost_estimate=pl.CostEstimate(flops=6 * 10**9, bytes_accessed=10 * 2**20, transcendentals=0),
    )(order, table, kernel_v, kernel_u, sources, target)


def solution(mesh):
    return jax.shard_map(
        on_device,
        mesh=mesh,
        in_specs=(
            P("freq", None, "tcol", None, None, None),
            P("freq", "tcol", None, None, None, None),
            P("freq", None, "tcol", None),
            P("freq", None, "tcol"),
            P(),
        ),
        out_specs=P("freq", "tcol", None, None),
        check_vma=False,
    )
```

```python
import jax
import jax.numpy as jnp
import numpy as np
from jax import lax
from jax.experimental import pallas as pl
from jax.experimental.pallas import tpu as pltpu
from jax.sharding import PartitionSpec as P

MESH = pl.DeviceIdType.MESH
NX, NY, NZ = 4, 4, 8
GROUPS = NX * NY
ROWS, COLS, SLOTS, TILE, WIDTH = 32, 4, 32, 256, 256
OWN = ROWS // GROUPS
PACK = 192
CHUNKS = 4
HALF = WIDTH // CHUNKS
LANES = 2 * HALF
DEPTH = GROUPS * PACK
BANDS = 2
BAND = TILE // BANDS

OFFSETS = (
    (2, 2), (2, 1), (1, 2), (2, 3), (3, 2), (1, 1), (3, 3), (1, 3), (3, 1),
    (2, 0), (0, 2), (1, 0), (3, 0), (0, 1), (0, 3),
)
PEERS = len(OFFSETS)


def swap_halves(v):
    return pltpu.roll(v, HALF, 1)


def kernel(
    owners, ranks, table, v_hbm, u_hbm, x_hbm, out,
    order, tgt, v, u, x, xs, coeff, packed, arrived, heads, left, acc,
    mine, theirs, near_out, near_in, far_out, far_in,
    load_sem, head_send, head_recv, tile_send, tile_recv, pair_send, pair_recv,
    near_send, near_recv, far_send, far_recv,
):
    freq, here = lax.axis_index("freq"), lax.axis_index("tcol")
    z, core = freq // 2, freq % 2
    px, py = here // NY, here % NY

    def load_v(j):
        return pltpu.make_async_copy(v_hbm.at[0, :, j], v.at[j], load_sem.at[2 + j])

    load_x = pltpu.make_async_copy(x_hbm.at[0], x, load_sem.at[0])
    load_u = pltpu.make_async_copy(u_hbm.at[0], u, load_sem.at[1])
    load_x.start()
    for j in range(COLS):
        load_v(j).start()
    load_u.start()

    def peer(k):
        dx, dy = OFFSETS[k]
        return ((px + dx) % NX) * NY + (py + dy) % NY

    sibling = (2 * z + 1 - core, here)
    sigma = 1 - 2 * core

    def along(steps):
        return (2 * ((z + sigma * steps + NZ) % NZ) + core, here)

    barrier = pltpu.get_barrier_semaphore()
    partners = [(freq, peer(k)) for k in range(PEERS)] + [sibling]
    partners += [along(steps) for steps in (1, -1, 2, -2, 3, -3)]
    for partner in partners:
        pl.semaphore_signal(barrier, inc=1, device_id=partner, device_id_type=MESH)

    def remote(src, dst, send, recv, device):
        return pltpu.make_async_remote_copy(
            src_ref=src, dst_ref=dst, send_sem=send, recv_sem=recv,
            device_id=device, device_id_type=MESH,
        )

    sub = lax.broadcasted_iota(jnp.int32, (8, COLS * SLOTS), 0)
    lane = lax.broadcasted_iota(jnp.int32, (8, COLS * SLOTS), 1)
    slot, column = lane % SLOTS, lane // SLOTS

    @pl.loop(0, GROUPS)
    def _(o):
        low, high = jnp.int32(ROWS - 1), jnp.int32(0)
        for i in range(ROWS):
            hit = owners[i] == o
            low = jnp.minimum(low, jnp.where(hit, i, ROWS - 1))
            high = jnp.maximum(high, jnp.where(hit, i, 0))
        start = jnp.int32(0)
        place = jnp.full((8, COLS * SLOTS), -1000, jnp.int32)
        for q, row in enumerate((low, high)):
            order[OWN * o + q] = row
            for j in range(COLS):
                rank = ranks[j, row]
                live = (sub == q) & (column == j) & (slot < rank)
                place = jnp.where(live, slot + start, place)
                start += rank
        tgt[o] = place.astype(jnp.float32)

    first = lax.broadcasted_iota(jnp.int32, (TILE, LANES), 1) < HALF
    rank_row = lax.broadcasted_iota(jnp.int32, (PACK, COLS * SLOTS), 0).astype(jnp.float32)
    my_rows = pl.ds(pl.multiple_of(PACK * here, PACK), PACK)
    head_rows = pl.ds(pl.multiple_of(8 * here, 8), 8)

    def head_copy(k):
        return remote(tgt.at[peer(k)], heads.at[head_rows], head_send.at[k], head_recv.at[k], (freq, peer(k)))

    def tile_copy(c, k):
        return remote(
            packed.at[c, k], arrived.at[c, my_rows], tile_send.at[c, k], tile_recv.at[c, k], (freq, peer(k))
        )

    def pack(owner):
        total = None
        for q in range(OWN):
            pick = jnp.where(rank_row == tgt[owner, q : q + 1, :], 1.0, 0.0).astype(jnp.bfloat16)
            part = jnp.dot(pick, coeff[order[OWN * owner + q]], preferred_element_type=jnp.float32)
            total = part if total is None else total + part
        return total.astype(jnp.bfloat16)

    load_x.wait()
    for half in range(CHUNKS // 2):
        lanes = pl.ds(half * LANES, LANES)

        @pl.loop(0, COLS)
        def _(j):
            rows = pl.ds(pl.multiple_of(j * TILE, TILE), TILE)
            re = x[0, rows, lanes].astype(jnp.float32)
            im = x[1, rows, lanes].astype(jnp.float32)
            re_swap, im_swap = swap_halves(re), swap_halves(im)
            xs[j, 0, :, :LANES] = jnp.where(first, re, im_swap).astype(jnp.bfloat16)
            xs[j, 0, :, LANES:] = jnp.where(first, re_swap, im).astype(jnp.bfloat16)
            xs[j, 1, :, :LANES] = jnp.where(first, im, -re_swap).astype(jnp.bfloat16)
            xs[j, 1, :, LANES:] = jnp.where(first, im_swap, -re).astype(jnp.bfloat16)

        @pl.loop(0, COLS)
        def _(j):
            if half == 0:
                load_v(j).wait()
            slot_rows = pl.ds(pl.multiple_of(j * SLOTS, SLOTS), SLOTS)
            for part in range(2):
                rows = pl.ds(part * (ROWS // 2), ROWS // 2)
                re = v[j, rows, 0].reshape(ROWS // 2 * SLOTS, TILE)
                im = v[j, rows, 1].reshape(ROWS // 2 * SLOTS, TILE)
                prod = jnp.dot(re, xs[j, 0], preferred_element_type=jnp.float32)
                prod += jnp.dot(im, xs[j, 1], preferred_element_type=jnp.float32)
                coeff[rows, slot_rows, :] = prod.astype(jnp.bfloat16).reshape(ROWS // 2, SLOTS, 2 * LANES)

        if half == 0:
            pl.semaphore_wait(barrier, len(partners))
        for k in range(PEERS):
            block = pack(peer(k))
            packed[2 * half, k] = block[:, :LANES]
            packed[2 * half + 1, k] = block[:, LANES:]
            tile_copy(2 * half, k).start()
        if half == 0:
            for k in range(PEERS):
                head_copy(k).start()
            heads[head_rows] = tgt[here]
        for k in range(PEERS):
            tile_copy(2 * half + 1, k).start()
        block = pack(here)
        arrived[2 * half, my_rows] = block[:, :LANES]
        arrived[2 * half + 1, my_rows] = block[:, LANES:]

    for k in range(PEERS):
        head_copy(k).wait_recv()
    load_u.wait()
    columns = jnp.transpose(heads[...])
    pair_row = lax.broadcasted_iota(jnp.int32, (COLS * SLOTS, 2 * PACK), 1).astype(jnp.float32)
    for e in range(GROUPS // 2):
        for q in range(OWN):
            sides = []
            for side in range(2):
                at = 8 * (2 * e + side) + q
                places = columns[:, at : at + 1] + float(side * PACK)
                sides.append(jnp.where(pair_row == places, 1.0, 0.0).astype(jnp.bfloat16))
            pick = jnp.concatenate(sides, axis=0)
            for a in range(2):
                block = u[q, 2 * COLS * e : 2 * COLS * (e + 1), a].reshape(2 * COLS * SLOTS, TILE)
                turned = lax.dot_general(block, pick, (((0,), (0,)), ((), ())), preferred_element_type=jnp.float32)
                turned = turned.astype(jnp.bfloat16)
                at = (2 * q + a) * BAND
                for t in range(BANDS):
                    left[t, at : at + BAND, 2 * PACK * e : 2 * PACK * (e + 1)] = turned[t * BAND : (t + 1) * BAND]

    head = first[:BAND]

    def pair_copy(c, t):
        return remote(mine.at[c, t], theirs.at[c, t], pair_send.at[c, t], pair_recv.at[c, t], sibling)

    def near_copy(c, t, n):
        rows, steps = ((pl.ds(0, 2), 1), (pl.ds(2, 1), -1), (pl.ds(3, 1), -1))[n]
        return remote(
            near_out.at[c, t, rows], near_in.at[c, t, rows], near_send.at[c, t, n], near_recv.at[c, t, n], along(steps)
        )

    def far_copy(c, t, n):
        return remote(
            far_out.at[c, t, n], far_in.at[c, t, n], far_send.at[c, t, n], far_recv.at[c, t, n], along((3, 1, -2)[n])
        )

    def share(c, t, steps):
        at = along(steps)[0] * (2 * NZ)
        own, other = at + freq, at + 2 * z + 1 - core
        shift = 4 * NZ * NZ
        return (
            table[own] * mine[c, t, 0] - table[own + shift] * mine[c, t, 1]
            + table[other] * theirs[c, t, 0] - table[other + shift] * theirs[c, t, 1]
        )

    def fields(c, t):
        acc[...] = jnp.dot(left[t], arrived[c], preferred_element_type=jnp.float32)
        parts = []
        for q in range(OWN):
            turned = swap_halves(acc[(2 * q + 1) * BAND : (2 * q + 2) * BAND])
            parts.append(acc[2 * q * BAND : (2 * q + 1) * BAND] + jnp.where(head, -turned, turned))
        mine[c, t, 0] = jnp.where(head, parts[0], swap_halves(parts[1]))
        mine[c, t, 1] = jnp.where(head, swap_halves(parts[0]), parts[1])
        pair_copy(c, t).start()

    def to_near(c, t):
        pair_copy(c, t).wait_recv()
        for n, steps in enumerate((4, 2, -3, -1)):
            near_out[c, t, n] = share(c, t, steps).astype(jnp.bfloat16)
            if n:
                near_copy(c, t, n - 1).start()

    def to_far(c, t):
        near_copy(c, t, 0).wait_recv()
        near_copy(c, t, 1).wait_recv()
        for n, steps in enumerate((3, 1, -2)):
            total = share(c, t, steps) + near_in[c, t, n].astype(jnp.float32)
            far_out[c, t, n] = total.astype(jnp.bfloat16)
            far_copy(c, t, n).start()

    def finish(c, t):
        near_copy(c, t, 2).wait_recv()
        total = share(c, t, 0) + near_in[c, t, 3].astype(jnp.float32)
        for n in (1, 2, 0):
            far_copy(c, t, n).wait_recv()
            total += far_in[c, t, n].astype(jnp.float32)
        turned = swap_halves(total)
        at = c * HALF
        rows = slice(t * BAND, (t + 1) * BAND)
        if c % 2 == 0:
            out[0, 0, rows, at : at + HALF] = total[:, :HALF]
            out[0, 1, rows, at : at + HALF] = turned[:, :HALF]
        else:
            out[0, 0, rows, at : at + HALF] = turned[:, HALF:]
            out[0, 1, rows, at : at + HALF] = total[:, HALF:]

    for c in range(CHUNKS):
        for k in range(PEERS):
            tile_copy(c, k).wait_recv()
        for t in range(BANDS):
            fields(c, t)
        for t in range(BANDS):
            to_near(c, t)
        for t in range(BANDS):
            if c:
                finish(c - 1, t)
        for t in range(BANDS):
            to_far(c, t)
    for t in range(BANDS):
        finish(CHUNKS - 1, t)

    for c in range(CHUNKS):
        for k in range(PEERS):
            tile_copy(c, k).wait_send()
        for t in range(BANDS):
            pair_copy(c, t).wait_send()
            for n in range(3):
                near_copy(c, t, n).wait_send()
                far_copy(c, t, n).wait_send()
    for k in range(PEERS):
        head_copy(k).wait_send()


def on_device(kernel_v, kernel_u, sources, ranks, row_owner):
    count = 2 * NZ
    phase = (np.arange(1, count + 1)[None, :] * np.arange(count)[:, None]) % (2 * count)
    angle = np.float32(np.pi) * phase.astype(np.float32) / np.float32(count)
    scale = np.float32(count ** (-0.5))
    table = np.concatenate([(np.cos(angle) * scale).reshape(-1), (np.sin(angle) * scale).reshape(-1)])

    bf16, f32 = jnp.bfloat16, jnp.float32
    vmem, dma = pltpu.VMEM, pltpu.SemaphoreType.DMA
    scalars = pl.BlockSpec(memory_space=pltpu.SMEM)
    away = pl.BlockSpec(memory_space=pl.ANY)
    rows, cols, parts, slots, tile = kernel_v.shape[1:]
    return pl.pallas_call(
        kernel,
        out_shape=jax.ShapeDtypeStruct((1, OWN, TILE, WIDTH), f32),
        in_specs=[scalars, scalars, scalars, away, away, away],
        out_specs=pl.BlockSpec(memory_space=pltpu.VMEM),
        scratch_shapes=[
            pltpu.SMEM((ROWS,), jnp.int32),
            vmem((GROUPS, 8, COLS * SLOTS), f32),
            vmem((cols, rows, parts, slots, tile), bf16),
            vmem(kernel_u.shape[1:], bf16),
            vmem(sources.shape[1:], bf16),
            vmem((COLS, 2, TILE, 2 * LANES), bf16),
            vmem((ROWS, COLS * SLOTS, 2 * LANES), bf16),
            vmem((CHUNKS, PEERS, PACK, LANES), bf16),
            vmem((CHUNKS, DEPTH, LANES), bf16),
            vmem((8 * GROUPS, COLS * SLOTS), f32),
            vmem((BANDS, 2 * OWN * BAND, DEPTH), bf16),
            vmem((2 * OWN * BAND, LANES), f32),
            vmem((CHUNKS, BANDS, 2, BAND, LANES), f32),
            vmem((CHUNKS, BANDS, 2, BAND, LANES), f32),
            vmem((CHUNKS, BANDS, 4, BAND, LANES), bf16),
            vmem((CHUNKS, BANDS, 4, BAND, LANES), bf16),
            vmem((CHUNKS, BANDS, 3, BAND, LANES), bf16),
            vmem((CHUNKS, BANDS, 3, BAND, LANES), bf16),
            dma((2 + COLS,)),
            dma((PEERS,)),
            dma((PEERS,)),
            dma((CHUNKS, PEERS)),
            dma((CHUNKS, PEERS)),
            dma((CHUNKS, BANDS)),
            dma((CHUNKS, BANDS)),
            dma((CHUNKS, BANDS, 3)),
            dma((CHUNKS, BANDS, 3)),
            dma((CHUNKS, BANDS, 3)),
            dma((CHUNKS, BANDS, 3)),
        ],
        compiler_params=pltpu.CompilerParams(
            collective_id=0, has_side_effects=True, vmem_limit_bytes=56 * 1024 * 1024
        ),
        cost_estimate=pl.CostEstimate(flops=6 * 10**9, bytes_accessed=10 * 2**20, transcendentals=0),
    )(row_owner, jnp.transpose(ranks[0]), table, kernel_v, kernel_u, sources)


def solution(mesh):
    return jax.shard_map(
        on_device,
        mesh=mesh,
        in_specs=(
            P("freq", None, "tcol", None, None, None),
            P("freq", "tcol", None, None, None, None),
            P("freq", None, "tcol", None),
            P("freq", None, "tcol"),
            P(),
        ),
        out_specs=P("freq", "tcol", None, None),
        check_vma=False,
    )
```

```python
import jax
import jax.numpy as jnp
import numpy as np
from jax import lax
from jax.experimental import pallas as pl
from jax.experimental.pallas import tpu as pltpu
from jax.sharding import PartitionSpec as P

MESH = pl.DeviceIdType.MESH
NX, NY, NZ = 4, 4, 8
GROUPS = NX * NY
ROWS, COLS, SLOTS, TILE, WIDTH = 32, 4, 32, 256, 256
OWN = ROWS // GROUPS
PACK = 192
CHUNKS = 4
HALF = WIDTH // CHUNKS
LANES = 2 * HALF
DEPTH = GROUPS * PACK
BANDS = 2
BAND = TILE // BANDS

OFFSETS = (
    (2, 2), (2, 1), (1, 2), (2, 3), (3, 2), (1, 1), (3, 3), (1, 3), (3, 1),
    (2, 0), (0, 2), (1, 0), (3, 0), (0, 1), (0, 3),
)
PEERS = len(OFFSETS)


def swap_halves(v):
    return pltpu.roll(v, HALF, 1)


def kernel(
    owners, ranks, table, v_hbm, u_hbm, x_hbm, out,
    order, tgt, v, u, x, xs, coeff, packed, arrived, heads, left, acc,
    mine, theirs, near_out, near_in, far_out, far_in,
    load_sem, head_send, head_recv, tile_send, tile_recv, pair_send, pair_recv,
    near_send, near_recv, far_send, far_recv,
):
    freq, here = lax.axis_index("freq"), lax.axis_index("tcol")
    z, core = freq // 2, freq % 2
    px, py = here // NY, here % NY

    def load_v(j):
        return pltpu.make_async_copy(v_hbm.at[0, :, j], v.at[j], load_sem.at[2 + j])

    load_x = pltpu.make_async_copy(x_hbm.at[0], x, load_sem.at[0])
    load_u = pltpu.make_async_copy(u_hbm.at[0], u, load_sem.at[1])
    load_x.start()
    for j in range(COLS):
        load_v(j).start()
    load_u.start()

    def peer(k):
        dx, dy = OFFSETS[k]
        return ((px + dx) % NX) * NY + (py + dy) % NY

    sibling = (2 * z + 1 - core, here)
    sigma = 1 - 2 * core

    def along(steps):
        return (2 * ((z + sigma * steps + NZ) % NZ) + core, here)

    barrier = pltpu.get_barrier_semaphore()
    partners = [(freq, peer(k)) for k in range(PEERS)] + [sibling]
    partners += [along(steps) for steps in (1, -1, 2, -2, 3, -3)]
    for partner in partners:
        pl.semaphore_signal(barrier, inc=1, device_id=partner, device_id_type=MESH)

    def remote(src, dst, send, recv, device):
        return pltpu.make_async_remote_copy(
            src_ref=src, dst_ref=dst, send_sem=send, recv_sem=recv,
            device_id=device, device_id_type=MESH,
        )

    sub = lax.broadcasted_iota(jnp.int32, (8, COLS * SLOTS), 0)
    lane = lax.broadcasted_iota(jnp.int32, (8, COLS * SLOTS), 1)
    slot, column = lane % SLOTS, lane // SLOTS

    @pl.loop(0, GROUPS)
    def _(o):
        low, high = jnp.int32(ROWS - 1), jnp.int32(0)
        for i in range(ROWS):
            hit = owners[i] == o
            low = jnp.minimum(low, jnp.where(hit, i, ROWS - 1))
            high = jnp.maximum(high, jnp.where(hit, i, 0))
        start = jnp.int32(0)
        place = jnp.full((8, COLS * SLOTS), -1000, jnp.int32)
        for q, row in enumerate((low, high)):
            order[OWN * o + q] = row
            for j in range(COLS):
                rank = ranks[j, row]
                live = (sub == q) & (column == j) & (slot < rank)
                place = jnp.where(live, slot + start, place)
                start += rank
        tgt[o] = place.astype(jnp.float32)

    first = lax.broadcasted_iota(jnp.int32, (TILE, LANES), 1) < HALF
    rank_row = lax.broadcasted_iota(jnp.int32, (PACK, COLS * SLOTS), 0).astype(jnp.float32)
    my_rows = pl.ds(pl.multiple_of(PACK * here, PACK), PACK)
    head_rows = pl.ds(pl.multiple_of(8 * here, 8), 8)

    def head_copy(k):
        return remote(tgt.at[peer(k)], heads.at[head_rows], head_send.at[k], head_recv.at[k], (freq, peer(k)))

    def tile_copy(c, k):
        return remote(
            packed.at[c, k], arrived.at[c, my_rows], tile_send.at[c, k], tile_recv.at[c, k], (freq, peer(k))
        )

    def pack(owner):
        total = None
        for q in range(OWN):
            pick = jnp.where(rank_row == tgt[owner, q : q + 1, :], 1.0, 0.0).astype(jnp.bfloat16)
            part = jnp.dot(pick, coeff[order[OWN * owner + q]], preferred_element_type=jnp.float32)
            total = part if total is None else total + part
        return total.astype(jnp.bfloat16)

    load_x.wait()
    for half in range(CHUNKS // 2):
        lanes = pl.ds(half * LANES, LANES)

        @pl.loop(0, COLS)
        def _(j):
            rows = pl.ds(pl.multiple_of(j * TILE, TILE), TILE)
            re = x[0, rows, lanes].astype(jnp.float32)
            im = x[1, rows, lanes].astype(jnp.float32)
            re_swap, im_swap = swap_halves(re), swap_halves(im)
            xs[j, 0, :, :LANES] = jnp.where(first, re, im_swap).astype(jnp.bfloat16)
            xs[j, 0, :, LANES:] = jnp.where(first, re_swap, im).astype(jnp.bfloat16)
            xs[j, 1, :, :LANES] = jnp.where(first, im, -re_swap).astype(jnp.bfloat16)
            xs[j, 1, :, LANES:] = jnp.where(first, im_swap, -re).astype(jnp.bfloat16)

        @pl.loop(0, COLS)
        def _(j):
            if half == 0:
                load_v(j).wait()
            slot_rows = pl.ds(pl.multiple_of(j * SLOTS, SLOTS), SLOTS)
            for part in range(2):
                rows = pl.ds(part * (ROWS // 2), ROWS // 2)
                re = v[j, rows, 0].reshape(ROWS // 2 * SLOTS, TILE)
                im = v[j, rows, 1].reshape(ROWS // 2 * SLOTS, TILE)
                prod = jnp.dot(re, xs[j, 0], preferred_element_type=jnp.float32)
                prod += jnp.dot(im, xs[j, 1], preferred_element_type=jnp.float32)
                coeff[rows, slot_rows, :] = prod.astype(jnp.bfloat16).reshape(ROWS // 2, SLOTS, 2 * LANES)

        if half == 0:
            pl.semaphore_wait(barrier, len(partners))
        for k in range(PEERS):
            block = pack(peer(k))
            packed[2 * half, k] = block[:, :LANES]
            packed[2 * half + 1, k] = block[:, LANES:]
            tile_copy(2 * half, k).start()
        if half == 0:
            for k in range(PEERS):
                head_copy(k).start()
            heads[head_rows] = tgt[here]
        for k in range(PEERS):
            tile_copy(2 * half + 1, k).start()
        block = pack(here)
        arrived[2 * half, my_rows] = block[:, :LANES]
        arrived[2 * half + 1, my_rows] = block[:, LANES:]

    for k in range(PEERS):
        head_copy(k).wait_recv()
    load_u.wait()
    columns = jnp.transpose(heads[...])
    pair_row = lax.broadcasted_iota(jnp.int32, (COLS * SLOTS, 2 * PACK), 1).astype(jnp.float32)
    for e in range(GROUPS // 2):
        for q in range(OWN):
            sides = []
            for side in range(2):
                at = 8 * (2 * e + side) + q
                places = columns[:, at : at + 1] + float(side * PACK)
                sides.append(jnp.where(pair_row == places, 1.0, 0.0).astype(jnp.bfloat16))
            pick = jnp.concatenate(sides, axis=0)
            for a in range(2):
                block = u[q, 2 * COLS * e : 2 * COLS * (e + 1), a].reshape(2 * COLS * SLOTS, TILE)
                turned = lax.dot_general(block, pick, (((0,), (0,)), ((), ())), preferred_element_type=jnp.float32)
                turned = turned.astype(jnp.bfloat16)
                at = (2 * q + a) * BAND
                for t in range(BANDS):
                    left[t, at : at + BAND, 2 * PACK * e : 2 * PACK * (e + 1)] = turned[t * BAND : (t + 1) * BAND]

    head = first[:BAND]

    def pair_copy(c, t):
        return remote(mine.at[c, t], theirs.at[c, t], pair_send.at[c, t], pair_recv.at[c, t], sibling)

    def near_copy(c, t, n):
        rows, steps = ((pl.ds(0, 2), 1), (pl.ds(2, 1), -1), (pl.ds(3, 1), -1))[n]
        return remote(
            near_out.at[c, t, rows], near_in.at[c, t, rows], near_send.at[c, t, n], near_recv.at[c, t, n], along(steps)
        )

    def far_copy(c, t, n):
        return remote(
            far_out.at[c, t, n], far_in.at[c, t, n], far_send.at[c, t, n], far_recv.at[c, t, n], along((3, 1, -2)[n])
        )

    def share(c, t, steps):
        at = along(steps)[0] * (2 * NZ)
        own, other = at + freq, at + 2 * z + 1 - core
        shift = 4 * NZ * NZ
        return (
            table[own] * mine[c, t, 0] - table[own + shift] * mine[c, t, 1]
            + table[other] * theirs[c, t, 0] - table[other + shift] * theirs[c, t, 1]
        )

    def fields(c, t):
        acc[...] = jnp.dot(left[t], arrived[c], preferred_element_type=jnp.float32)
        parts = []
        for q in range(OWN):
            turned = swap_halves(acc[(2 * q + 1) * BAND : (2 * q + 2) * BAND])
            parts.append(acc[2 * q * BAND : (2 * q + 1) * BAND] + jnp.where(head, -turned, turned))
        mine[c, t, 0] = jnp.where(head, parts[0], swap_halves(parts[1]))
        mine[c, t, 1] = jnp.where(head, swap_halves(parts[0]), parts[1])
        pair_copy(c, t).start()

    def to_near(c, t):
        pair_copy(c, t).wait_recv()
        for n, steps in enumerate((4, 2, -3, -1)):
            near_out[c, t, n] = share(c, t, steps).astype(jnp.bfloat16)
            if n:
                near_copy(c, t, n - 1).start()

    def to_far(c, t):
        near_copy(c, t, 0).wait_recv()
        near_copy(c, t, 1).wait_recv()
        for n, steps in enumerate((3, 1, -2)):
            total = share(c, t, steps) + near_in[c, t, n].astype(jnp.float32)
            far_out[c, t, n] = total.astype(jnp.bfloat16)
            far_copy(c, t, n).start()

    def finish(c, t):
        near_copy(c, t, 2).wait_recv()
        total = share(c, t, 0) + near_in[c, t, 3].astype(jnp.float32)
        for n in (1, 2, 0):
            far_copy(c, t, n).wait_recv()
            total += far_in[c, t, n].astype(jnp.float32)
        turned = swap_halves(total)
        at = c * HALF
        rows = slice(t * BAND, (t + 1) * BAND)
        if c % 2 == 0:
            out[0, 0, rows, at : at + HALF] = total[:, :HALF]
            out[0, 1, rows, at : at + HALF] = turned[:, :HALF]
        else:
            out[0, 0, rows, at : at + HALF] = turned[:, HALF:]
            out[0, 1, rows, at : at + HALF] = total[:, HALF:]

    for c in range(CHUNKS):
        for k in range(PEERS):
            tile_copy(c, k).wait_recv()
        for t in range(BANDS):
            fields(c, t)
        for t in range(BANDS):
            if c:
                to_far(c - 1, t)
        for t in range(BANDS):
            to_near(c, t)
        for t in range(BANDS):
            if c > 1:
                finish(c - 2, t)
    for t in range(BANDS):
        finish(CHUNKS - 2, t)
    for t in range(BANDS):
        to_far(CHUNKS - 1, t)
    for t in range(BANDS):
        finish(CHUNKS - 1, t)

    for c in range(CHUNKS):
        for k in range(PEERS):
            tile_copy(c, k).wait_send()
        for t in range(BANDS):
            pair_copy(c, t).wait_send()
            for n in range(3):
                near_copy(c, t, n).wait_send()
                far_copy(c, t, n).wait_send()
    for k in range(PEERS):
        head_copy(k).wait_send()


def on_device(kernel_v, kernel_u, sources, ranks, row_owner):
    count = 2 * NZ
    phase = (np.arange(1, count + 1)[None, :] * np.arange(count)[:, None]) % (2 * count)
    angle = np.float32(np.pi) * phase.astype(np.float32) / np.float32(count)
    scale = np.float32(count ** (-0.5))
    table = np.concatenate([(np.cos(angle) * scale).reshape(-1), (np.sin(angle) * scale).reshape(-1)])

    bf16, f32 = jnp.bfloat16, jnp.float32
    vmem, dma = pltpu.VMEM, pltpu.SemaphoreType.DMA
    scalars = pl.BlockSpec(memory_space=pltpu.SMEM)
    away = pl.BlockSpec(memory_space=pl.ANY)
    rows, cols, parts, slots, tile = kernel_v.shape[1:]
    return pl.pallas_call(
        kernel,
        out_shape=jax.ShapeDtypeStruct((1, OWN, TILE, WIDTH), f32),
        in_specs=[scalars, scalars, scalars, away, away, away],
        out_specs=pl.BlockSpec(memory_space=pltpu.VMEM),
        scratch_shapes=[
            pltpu.SMEM((ROWS,), jnp.int32),
            vmem((GROUPS, 8, COLS * SLOTS), f32),
            vmem((cols, rows, parts, slots, tile), bf16),
            vmem(kernel_u.shape[1:], bf16),
            vmem(sources.shape[1:], bf16),
            vmem((COLS, 2, TILE, 2 * LANES), bf16),
            vmem((ROWS, COLS * SLOTS, 2 * LANES), bf16),
            vmem((CHUNKS, PEERS, PACK, LANES), bf16),
            vmem((CHUNKS, DEPTH, LANES), bf16),
            vmem((8 * GROUPS, COLS * SLOTS), f32),
            vmem((BANDS, 2 * OWN * BAND, DEPTH), bf16),
            vmem((2 * OWN * BAND, LANES), f32),
            vmem((CHUNKS, BANDS, 2, BAND, LANES), f32),
            vmem((CHUNKS, BANDS, 2, BAND, LANES), f32),
            vmem((CHUNKS, BANDS, 4, BAND, LANES), bf16),
            vmem((CHUNKS, BANDS, 4, BAND, LANES), bf16),
            vmem((CHUNKS, BANDS, 3, BAND, LANES), bf16),
            vmem((CHUNKS, BANDS, 3, BAND, LANES), bf16),
            dma((2 + COLS,)),
            dma((PEERS,)),
            dma((PEERS,)),
            dma((CHUNKS, PEERS)),
            dma((CHUNKS, PEERS)),
            dma((CHUNKS, BANDS)),
            dma((CHUNKS, BANDS)),
            dma((CHUNKS, BANDS, 3)),
            dma((CHUNKS, BANDS, 3)),
            dma((CHUNKS, BANDS, 3)),
            dma((CHUNKS, BANDS, 3)),
        ],
        compiler_params=pltpu.CompilerParams(
            collective_id=0, has_side_effects=True, vmem_limit_bytes=56 * 1024 * 1024
        ),
        cost_estimate=pl.CostEstimate(flops=6 * 10**9, bytes_accessed=10 * 2**20, transcendentals=0),
    )(row_owner, jnp.transpose(ranks[0]), table, kernel_v, kernel_u, sources)


def solution(mesh):
    return jax.shard_map(
        on_device,
        mesh=mesh,
        in_specs=(
            P("freq", None, "tcol", None, None, None),
            P("freq", "tcol", None, None, None, None),
            P("freq", None, "tcol", None),
            P("freq", None, "tcol"),
            P(),
        ),
        out_specs=P("freq", "tcol", None, None),
        check_vma=False,
    )
```

```python
import jax
import jax.numpy as jnp
import numpy as np
from jax import lax
from jax.experimental import pallas as pl
from jax.experimental.pallas import tpu as pltpu
from jax.sharding import PartitionSpec as P

MESH = pl.DeviceIdType.MESH
NX, NY, NZ = 4, 4, 8
GROUPS = NX * NY
ROWS, COLS, SLOTS, TILE, WIDTH = 32, 4, 32, 256, 256
OWN = ROWS // GROUPS
PACK = 192
CHUNKS = 4
HALF = WIDTH // CHUNKS
LANES = 2 * HALF
DEPTH = GROUPS * PACK
BANDS = 4
BAND = TILE // BANDS

OFFSETS = (
    (2, 2), (2, 1), (1, 2), (2, 3), (3, 2), (1, 1), (3, 3), (1, 3), (3, 1),
    (2, 0), (0, 2), (1, 0), (3, 0), (0, 1), (0, 3),
)
PEERS = len(OFFSETS)


def swap_halves(v):
    return pltpu.roll(v, HALF, 1)


def kernel(
    owners, ranks, table, v_hbm, u_hbm, x_hbm, out,
    order, tgt, v, u, x, xs, coeff, packed, arrived, heads, left, acc,
    mine, theirs, near_out, near_in, far_out, far_in,
    load_sem, head_send, head_recv, tile_send, tile_recv, pair_send, pair_recv,
    near_send, near_recv, far_send, far_recv,
):
    freq, here = lax.axis_index("freq"), lax.axis_index("tcol")
    z, core = freq // 2, freq % 2
    px, py = here // NY, here % NY

    def load_v(j):
        return pltpu.make_async_copy(v_hbm.at[0, :, j], v.at[j], load_sem.at[2 + j])

    load_x = pltpu.make_async_copy(x_hbm.at[0], x, load_sem.at[0])
    load_u = pltpu.make_async_copy(u_hbm.at[0], u, load_sem.at[1])
    load_x.start()
    for j in range(COLS):
        load_v(j).start()
    load_u.start()

    def peer(k):
        dx, dy = OFFSETS[k]
        return ((px + dx) % NX) * NY + (py + dy) % NY

    sibling = (2 * z + 1 - core, here)
    sigma = 1 - 2 * core

    def along(steps):
        return (2 * ((z + sigma * steps + NZ) % NZ) + core, here)

    barrier = pltpu.get_barrier_semaphore()
    partners = [(freq, peer(k)) for k in range(PEERS)] + [sibling]
    partners += [along(steps) for steps in (1, -1, 2, -2, 3, -3)]
    for partner in partners:
        pl.semaphore_signal(barrier, inc=1, device_id=partner, device_id_type=MESH)

    def remote(src, dst, send, recv, device):
        return pltpu.make_async_remote_copy(
            src_ref=src, dst_ref=dst, send_sem=send, recv_sem=recv,
            device_id=device, device_id_type=MESH,
        )

    sub = lax.broadcasted_iota(jnp.int32, (8, COLS * SLOTS), 0)
    lane = lax.broadcasted_iota(jnp.int32, (8, COLS * SLOTS), 1)
    slot, column = lane % SLOTS, lane // SLOTS

    @pl.loop(0, GROUPS)
    def _(o):
        low, high = jnp.int32(ROWS - 1), jnp.int32(0)
        for i in range(ROWS):
            hit = owners[i] == o
            low = jnp.minimum(low, jnp.where(hit, i, ROWS - 1))
            high = jnp.maximum(high, jnp.where(hit, i, 0))
        start = jnp.int32(0)
        place = jnp.full((8, COLS * SLOTS), -1000, jnp.int32)
        for q, row in enumerate((low, high)):
            order[OWN * o + q] = row
            for j in range(COLS):
                rank = ranks[j, row]
                live = (sub == q) & (column == j) & (slot < rank)
                place = jnp.where(live, slot + start, place)
                start += rank
        tgt[o] = place.astype(jnp.float32)

    first = lax.broadcasted_iota(jnp.int32, (TILE, LANES), 1) < HALF
    rank_row = lax.broadcasted_iota(jnp.int32, (PACK, COLS * SLOTS), 0).astype(jnp.float32)
    my_rows = pl.ds(pl.multiple_of(PACK * here, PACK), PACK)
    head_rows = pl.ds(pl.multiple_of(8 * here, 8), 8)

    def head_copy(k):
        return remote(tgt.at[peer(k)], heads.at[head_rows], head_send.at[k], head_recv.at[k], (freq, peer(k)))

    def tile_copy(c, k):
        return remote(
            packed.at[c, k], arrived.at[c, my_rows], tile_send.at[c, k], tile_recv.at[c, k], (freq, peer(k))
        )

    def pack(owner):
        total = None
        for q in range(OWN):
            pick = jnp.where(rank_row == tgt[owner, q : q + 1, :], 1.0, 0.0).astype(jnp.bfloat16)
            part = jnp.dot(pick, coeff[order[OWN * owner + q]], preferred_element_type=jnp.float32)
            total = part if total is None else total + part
        return total.astype(jnp.bfloat16)

    load_x.wait()
    for half in range(CHUNKS // 2):
        lanes = pl.ds(half * LANES, LANES)

        @pl.loop(0, COLS)
        def _(j):
            rows = pl.ds(pl.multiple_of(j * TILE, TILE), TILE)
            re = x[0, rows, lanes].astype(jnp.float32)
            im = x[1, rows, lanes].astype(jnp.float32)
            re_swap, im_swap = swap_halves(re), swap_halves(im)
            xs[j, 0, :, :LANES] = jnp.where(first, re, im_swap).astype(jnp.bfloat16)
            xs[j, 0, :, LANES:] = jnp.where(first, re_swap, im).astype(jnp.bfloat16)
            xs[j, 1, :, :LANES] = jnp.where(first, im, -re_swap).astype(jnp.bfloat16)
            xs[j, 1, :, LANES:] = jnp.where(first, im_swap, -re).astype(jnp.bfloat16)

        @pl.loop(0, COLS)
        def _(j):
            if half == 0:
                load_v(j).wait()
            slot_rows = pl.ds(pl.multiple_of(j * SLOTS, SLOTS), SLOTS)
            for part in range(2):
                rows = pl.ds(part * (ROWS // 2), ROWS // 2)
                re = v[j, rows, 0].reshape(ROWS // 2 * SLOTS, TILE)
                im = v[j, rows, 1].reshape(ROWS // 2 * SLOTS, TILE)
                prod = jnp.dot(re, xs[j, 0], preferred_element_type=jnp.float32)
                prod += jnp.dot(im, xs[j, 1], preferred_element_type=jnp.float32)
                coeff[rows, slot_rows, :] = prod.astype(jnp.bfloat16).reshape(ROWS // 2, SLOTS, 2 * LANES)

        if half == 0:
            pl.semaphore_wait(barrier, len(partners))
        for k in range(PEERS):
            block = pack(peer(k))
            packed[2 * half, k] = block[:, :LANES]
            packed[2 * half + 1, k] = block[:, LANES:]
            tile_copy(2 * half, k).start()
        if half == 0:
            for k in range(PEERS):
                head_copy(k).start()
            heads[head_rows] = tgt[here]
        for k in range(PEERS):
            tile_copy(2 * half + 1, k).start()
        block = pack(here)
        arrived[2 * half, my_rows] = block[:, :LANES]
        arrived[2 * half + 1, my_rows] = block[:, LANES:]

    for k in range(PEERS):
        head_copy(k).wait_recv()
    load_u.wait()
    columns = jnp.transpose(heads[...])
    pair_row = lax.broadcasted_iota(jnp.int32, (COLS * SLOTS, 2 * PACK), 1).astype(jnp.float32)
    for e in range(GROUPS // 2):
        for q in range(OWN):
            sides = []
            for side in range(2):
                at = 8 * (2 * e + side) + q
                places = columns[:, at : at + 1] + float(side * PACK)
                sides.append(jnp.where(pair_row == places, 1.0, 0.0).astype(jnp.bfloat16))
            pick = jnp.concatenate(sides, axis=0)
            for a in range(2):
                block = u[q, 2 * COLS * e : 2 * COLS * (e + 1), a].reshape(2 * COLS * SLOTS, TILE)
                turned = lax.dot_general(block, pick, (((0,), (0,)), ((), ())), preferred_element_type=jnp.float32)
                turned = turned.astype(jnp.bfloat16)
                at = (2 * q + a) * BAND
                for t in range(BANDS):
                    left[t, at : at + BAND, 2 * PACK * e : 2 * PACK * (e + 1)] = turned[t * BAND : (t + 1) * BAND]

    head = first[:BAND]

    def pair_copy(c, t):
        return remote(mine.at[c, t], theirs.at[c, t], pair_send.at[c, t], pair_recv.at[c, t], sibling)

    def near_copy(c, t, n):
        rows, steps = ((pl.ds(0, 2), 1), (pl.ds(2, 1), -1), (pl.ds(3, 1), -1))[n]
        return remote(
            near_out.at[c, t, rows], near_in.at[c, t, rows], near_send.at[c, t, n], near_recv.at[c, t, n], along(steps)
        )

    def far_copy(c, t, n):
        return remote(
            far_out.at[c, t, n], far_in.at[c, t, n], far_send.at[c, t, n], far_recv.at[c, t, n], along((3, 1, -2)[n])
        )

    def share(c, t, steps):
        at = along(steps)[0] * (2 * NZ)
        own, other = at + freq, at + 2 * z + 1 - core
        shift = 4 * NZ * NZ
        return (
            table[own] * mine[c, t, 0] - table[own + shift] * mine[c, t, 1]
            + table[other] * theirs[c, t, 0] - table[other + shift] * theirs[c, t, 1]
        )

    def fields(c, t):
        acc[...] = jnp.dot(left[t], arrived[c], preferred_element_type=jnp.float32)
        parts = []
        for q in range(OWN):
            turned = swap_halves(acc[(2 * q + 1) * BAND : (2 * q + 2) * BAND])
            parts.append(acc[2 * q * BAND : (2 * q + 1) * BAND] + jnp.where(head, -turned, turned))
        mine[c, t, 0] = jnp.where(head, parts[0], swap_halves(parts[1]))
        mine[c, t, 1] = jnp.where(head, swap_halves(parts[0]), parts[1])
        pair_copy(c, t).start()

    def to_near(c, t):
        pair_copy(c, t).wait_recv()
        for n, steps in enumerate((4, 2, -3, -1)):
            near_out[c, t, n] = share(c, t, steps).astype(jnp.bfloat16)
            if n:
                near_copy(c, t, n - 1).start()

    def to_far(c, t):
        near_copy(c, t, 0).wait_recv()
        near_copy(c, t, 1).wait_recv()
        for n, steps in enumerate((3, 1, -2)):
            total = share(c, t, steps) + near_in[c, t, n].astype(jnp.float32)
            far_out[c, t, n] = total.astype(jnp.bfloat16)
            far_copy(c, t, n).start()

    def finish(c, t):
        near_copy(c, t, 2).wait_recv()
        total = share(c, t, 0) + near_in[c, t, 3].astype(jnp.float32)
        for n in (1, 2, 0):
            far_copy(c, t, n).wait_recv()
            total += far_in[c, t, n].astype(jnp.float32)
        turned = swap_halves(total)
        at = c * HALF
        rows = slice(t * BAND, (t + 1) * BAND)
        if c % 2 == 0:
            out[0, 0, rows, at : at + HALF] = total[:, :HALF]
            out[0, 1, rows, at : at + HALF] = turned[:, :HALF]
        else:
            out[0, 0, rows, at : at + HALF] = turned[:, HALF:]
            out[0, 1, rows, at : at + HALF] = total[:, HALF:]

    for c in range(CHUNKS):
        for k in range(PEERS):
            tile_copy(c, k).wait_recv()
        for t in range(BANDS):
            fields(c, t)
        for t in range(BANDS):
            if c:
                to_far(c - 1, t)
        for t in range(BANDS):
            to_near(c, t)
        for t in range(BANDS):
            if c > 1:
                finish(c - 2, t)
    for t in range(BANDS):
        finish(CHUNKS - 2, t)
    for t in range(BANDS):
        to_far(CHUNKS - 1, t)
    for t in range(BANDS):
        finish(CHUNKS - 1, t)

    for c in range(CHUNKS):
        for k in range(PEERS):
            tile_copy(c, k).wait_send()
        for t in range(BANDS):
            pair_copy(c, t).wait_send()
            for n in range(3):
                near_copy(c, t, n).wait_send()
                far_copy(c, t, n).wait_send()
    for k in range(PEERS):
        head_copy(k).wait_send()


def on_device(kernel_v, kernel_u, sources, ranks, row_owner):
    count = 2 * NZ
    phase = (np.arange(1, count + 1)[None, :] * np.arange(count)[:, None]) % (2 * count)
    angle = np.float32(np.pi) * phase.astype(np.float32) / np.float32(count)
    scale = np.float32(count ** (-0.5))
    table = np.concatenate([(np.cos(angle) * scale).reshape(-1), (np.sin(angle) * scale).reshape(-1)])

    bf16, f32 = jnp.bfloat16, jnp.float32
    vmem, dma = pltpu.VMEM, pltpu.SemaphoreType.DMA
    scalars = pl.BlockSpec(memory_space=pltpu.SMEM)
    away = pl.BlockSpec(memory_space=pl.ANY)
    rows, cols, parts, slots, tile = kernel_v.shape[1:]
    return pl.pallas_call(
        kernel,
        out_shape=jax.ShapeDtypeStruct((1, OWN, TILE, WIDTH), f32),
        in_specs=[scalars, scalars, scalars, away, away, away],
        out_specs=pl.BlockSpec(memory_space=pltpu.VMEM),
        scratch_shapes=[
            pltpu.SMEM((ROWS,), jnp.int32),
            vmem((GROUPS, 8, COLS * SLOTS), f32),
            vmem((cols, rows, parts, slots, tile), bf16),
            vmem(kernel_u.shape[1:], bf16),
            vmem(sources.shape[1:], bf16),
            vmem((COLS, 2, TILE, 2 * LANES), bf16),
            vmem((ROWS, COLS * SLOTS, 2 * LANES), bf16),
            vmem((CHUNKS, PEERS, PACK, LANES), bf16),
            vmem((CHUNKS, DEPTH, LANES), bf16),
            vmem((8 * GROUPS, COLS * SLOTS), f32),
            vmem((BANDS, 2 * OWN * BAND, DEPTH), bf16),
            vmem((2 * OWN * BAND, LANES), f32),
            vmem((CHUNKS, BANDS, 2, BAND, LANES), f32),
            vmem((CHUNKS, BANDS, 2, BAND, LANES), f32),
            vmem((CHUNKS, BANDS, 4, BAND, LANES), bf16),
            vmem((CHUNKS, BANDS, 4, BAND, LANES), bf16),
            vmem((CHUNKS, BANDS, 3, BAND, LANES), bf16),
            vmem((CHUNKS, BANDS, 3, BAND, LANES), bf16),
            dma((2 + COLS,)),
            dma((PEERS,)),
            dma((PEERS,)),
            dma((CHUNKS, PEERS)),
            dma((CHUNKS, PEERS)),
            dma((CHUNKS, BANDS)),
            dma((CHUNKS, BANDS)),
            dma((CHUNKS, BANDS, 3)),
            dma((CHUNKS, BANDS, 3)),
            dma((CHUNKS, BANDS, 3)),
            dma((CHUNKS, BANDS, 3)),
        ],
        compiler_params=pltpu.CompilerParams(
            collective_id=0, has_side_effects=True, vmem_limit_bytes=56 * 1024 * 1024
        ),
        cost_estimate=pl.CostEstimate(flops=6 * 10**9, bytes_accessed=10 * 2**20, transcendentals=0),
    )(row_owner, jnp.transpose(ranks[0]), table, kernel_v, kernel_u, sources)


def solution(mesh):
    return jax.shard_map(
        on_device,
        mesh=mesh,
        in_specs=(
            P("freq", None, "tcol", None, None, None),
            P("freq", "tcol", None, None, None, None),
            P("freq", None, "tcol", None),
            P("freq", None, "tcol"),
            P(),
        ),
        out_specs=P("freq", "tcol", None, None),
        check_vma=False,
    )
```

```python
import jax
import jax.numpy as jnp
import numpy as np
from jax import lax
from jax.experimental import pallas as pl
from jax.experimental.pallas import tpu as pltpu
from jax.sharding import PartitionSpec as P

MESH = pl.DeviceIdType.MESH
NX, NY, NZ = 4, 4, 8
GROUPS = NX * NY
ROWS, COLS, SLOTS, TILE, WIDTH = 32, 4, 32, 256, 256
OWN = ROWS // GROUPS
PACK = 192
CHUNKS = 4
HALF = WIDTH // CHUNKS
LANES = 2 * HALF
DEPTH = GROUPS * PACK
BANDS = 4
BAND = TILE // BANDS

OFFSETS = (
    (2, 2), (2, 1), (1, 2), (2, 3), (3, 2), (1, 1), (3, 3), (1, 3), (3, 1),
    (2, 0), (0, 2), (1, 0), (3, 0), (0, 1), (0, 3),
)
PEERS = len(OFFSETS)


def swap_halves(v):
    return pltpu.roll(v, HALF, 1)


def kernel(
    owners, ranks, table, v_hbm, u_hbm, x_hbm, out,
    order, tgt, v, u, x, xs, coeff, packed, arrived, heads, left, acc,
    mine, theirs, near_out, near_in, far_out, far_in,
    load_sem, head_send, head_recv, tile_send, tile_recv, pair_send, pair_recv,
    near_send, near_recv, far_send, far_recv,
):
    freq, here = lax.axis_index("freq"), lax.axis_index("tcol")
    z, core = freq // 2, freq % 2
    px, py = here // NY, here % NY

    def load_v(j):
        return pltpu.make_async_copy(v_hbm.at[0, :, j], v.at[j], load_sem.at[2 + j])

    load_x = pltpu.make_async_copy(x_hbm.at[0], x, load_sem.at[0])
    load_u = pltpu.make_async_copy(u_hbm.at[0], u, load_sem.at[1])
    load_x.start()
    for j in range(COLS):
        load_v(j).start()
    load_u.start()

    def peer(k):
        dx, dy = OFFSETS[k]
        return ((px + dx) % NX) * NY + (py + dy) % NY

    sibling = (2 * z + 1 - core, here)
    sigma = 1 - 2 * core

    def along(steps):
        return (2 * ((z + sigma * steps + NZ) % NZ) + core, here)

    barrier = pltpu.get_barrier_semaphore()
    partners = [(freq, peer(k)) for k in range(PEERS)] + [sibling]
    partners += [along(steps) for steps in (1, -1, 2, -2, 3, -3)]
    for partner in partners:
        pl.semaphore_signal(barrier, inc=1, device_id=partner, device_id_type=MESH)

    def remote(src, dst, send, recv, device):
        return pltpu.make_async_remote_copy(
            src_ref=src, dst_ref=dst, send_sem=send, recv_sem=recv,
            device_id=device, device_id_type=MESH,
        )

    sub = lax.broadcasted_iota(jnp.int32, (8, COLS * SLOTS), 0)
    lane = lax.broadcasted_iota(jnp.int32, (8, COLS * SLOTS), 1)
    slot, column = lane % SLOTS, lane // SLOTS

    @pl.loop(0, GROUPS)
    def _(o):
        low, high = jnp.int32(ROWS - 1), jnp.int32(0)
        for i in range(ROWS):
            hit = owners[i] == o
            low = jnp.minimum(low, jnp.where(hit, i, ROWS - 1))
            high = jnp.maximum(high, jnp.where(hit, i, 0))
        start = jnp.int32(0)
        place = jnp.full((8, COLS * SLOTS), -1000, jnp.int32)
        for q, row in enumerate((low, high)):
            order[OWN * o + q] = row
            for j in range(COLS):
                rank = ranks[j, row]
                live = (sub == q) & (column == j) & (slot < rank)
                place = jnp.where(live, slot + start, place)
                start += rank
        tgt[o] = place.astype(jnp.float32)

    first = lax.broadcasted_iota(jnp.int32, (TILE, LANES), 1) < HALF
    rank_row = lax.broadcasted_iota(jnp.int32, (PACK, COLS * SLOTS), 0).astype(jnp.float32)
    my_rows = pl.ds(pl.multiple_of(PACK * here, PACK), PACK)
    head_rows = pl.ds(pl.multiple_of(8 * here, 8), 8)

    def head_copy(k):
        return remote(tgt.at[peer(k)], heads.at[head_rows], head_send.at[k], head_recv.at[k], (freq, peer(k)))

    def tile_copy(c, k):
        return remote(
            packed.at[c, k], arrived.at[c, my_rows], tile_send.at[c, k], tile_recv.at[c, k], (freq, peer(k))
        )

    def pack(owner):
        total = None
        for q in range(OWN):
            pick = jnp.where(rank_row == tgt[owner, q : q + 1, :], 1.0, 0.0).astype(jnp.bfloat16)
            part = jnp.dot(pick, coeff[order[OWN * owner + q]], preferred_element_type=jnp.float32)
            total = part if total is None else total + part
        return total.astype(jnp.bfloat16)

    load_x.wait()
    for half in range(CHUNKS // 2):
        lanes = pl.ds(half * LANES, LANES)

        @pl.loop(0, COLS)
        def _(j):
            rows = pl.ds(pl.multiple_of(j * TILE, TILE), TILE)
            re = x[0, rows, lanes].astype(jnp.float32)
            im = x[1, rows, lanes].astype(jnp.float32)
            re_swap, im_swap = swap_halves(re), swap_halves(im)
            xs[j, 0, :, :LANES] = jnp.where(first, re, im_swap).astype(jnp.bfloat16)
            xs[j, 0, :, LANES:] = jnp.where(first, re_swap, im).astype(jnp.bfloat16)
            xs[j, 1, :, :LANES] = jnp.where(first, im, -re_swap).astype(jnp.bfloat16)
            xs[j, 1, :, LANES:] = jnp.where(first, im_swap, -re).astype(jnp.bfloat16)

        @pl.loop(0, COLS)
        def _(j):
            if half == 0:
                load_v(j).wait()
            slot_rows = pl.ds(pl.multiple_of(j * SLOTS, SLOTS), SLOTS)
            for part in range(2):
                rows = pl.ds(part * (ROWS // 2), ROWS // 2)
                re = v[j, rows, 0].reshape(ROWS // 2 * SLOTS, TILE)
                im = v[j, rows, 1].reshape(ROWS // 2 * SLOTS, TILE)
                prod = jnp.dot(re, xs[j, 0], preferred_element_type=jnp.float32)
                prod += jnp.dot(im, xs[j, 1], preferred_element_type=jnp.float32)
                coeff[rows, slot_rows, :] = prod.astype(jnp.bfloat16).reshape(ROWS // 2, SLOTS, 2 * LANES)

        if half == 0:
            pl.semaphore_wait(barrier, len(partners))
        for k in range(PEERS):
            block = pack(peer(k))
            packed[2 * half, k] = block[:, :LANES]
            packed[2 * half + 1, k] = block[:, LANES:]
            tile_copy(2 * half, k).start()
        if half == 0:
            for k in range(PEERS):
                head_copy(k).start()
            heads[head_rows] = tgt[here]
        for k in range(PEERS):
            tile_copy(2 * half + 1, k).start()
        block = pack(here)
        arrived[2 * half, my_rows] = block[:, :LANES]
        arrived[2 * half + 1, my_rows] = block[:, LANES:]

    for k in range(PEERS):
        head_copy(k).wait_recv()
    load_u.wait()
    columns = jnp.transpose(heads[...])
    pair_row = lax.broadcasted_iota(jnp.int32, (COLS * SLOTS, 2 * PACK), 1).astype(jnp.float32)
    for e in range(GROUPS // 2):
        for q in range(OWN):
            sides = []
            for side in range(2):
                at = 8 * (2 * e + side) + q
                places = columns[:, at : at + 1] + float(side * PACK)
                sides.append(jnp.where(pair_row == places, 1.0, 0.0).astype(jnp.bfloat16))
            pick = jnp.concatenate(sides, axis=0)
            for a in range(2):
                block = u[q, 2 * COLS * e : 2 * COLS * (e + 1), a].reshape(2 * COLS * SLOTS, TILE)
                turned = lax.dot_general(block, pick, (((0,), (0,)), ((), ())), preferred_element_type=jnp.float32)
                turned = turned.astype(jnp.bfloat16)
                at = (2 * q + a) * BAND
                for t in range(BANDS):
                    left[t, at : at + BAND, 2 * PACK * e : 2 * PACK * (e + 1)] = turned[t * BAND : (t + 1) * BAND]

    head = first[:BAND]

    def pair_copy(c, t):
        return remote(mine.at[c, t], theirs.at[c, t], pair_send.at[c, t], pair_recv.at[c, t], sibling)

    def near_copy(c, t, n):
        rows, steps = ((pl.ds(0, 2), 1), (pl.ds(2, 1), -1), (pl.ds(3, 1), -1))[n]
        return remote(
            near_out.at[c, t, rows], near_in.at[c, t, rows], near_send.at[c, t, n], near_recv.at[c, t, n], along(steps)
        )

    def far_copy(c, t, n):
        return remote(
            far_out.at[c, t, n], far_in.at[c, t, n], far_send.at[c, t, n], far_recv.at[c, t, n], along((3, 1, -2)[n])
        )

    def share(c, t, steps):
        at = along(steps)[0] * (2 * NZ)
        own, other = at + freq, at + 2 * z + 1 - core
        shift = 4 * NZ * NZ
        return (
            table[own] * mine[c, t, 0] - table[own + shift] * mine[c, t, 1]
            + table[other] * theirs[c, t, 0] - table[other + shift] * theirs[c, t, 1]
        )

    def fields(c, t):
        acc[...] = jnp.dot(left[t], arrived[c], preferred_element_type=jnp.float32)
        parts = []
        for q in range(OWN):
            turned = swap_halves(acc[(2 * q + 1) * BAND : (2 * q + 2) * BAND])
            parts.append(acc[2 * q * BAND : (2 * q + 1) * BAND] + jnp.where(head, -turned, turned))
        mine[c, t, 0] = jnp.where(head, parts[0], swap_halves(parts[1]))
        mine[c, t, 1] = jnp.where(head, swap_halves(parts[0]), parts[1])
        pair_copy(c, t).start()

    def to_near(c, t):
        pair_copy(c, t).wait_recv()
        for n, steps in enumerate((4, 2, -3, -1)):
            near_out[c, t, n] = share(c, t, steps).astype(jnp.bfloat16)
            if n:
                near_copy(c, t, n - 1).start()

    def to_far(c, t):
        near_copy(c, t, 0).wait_recv()
        near_copy(c, t, 1).wait_recv()
        for n, steps in enumerate((3, 1, -2)):
            total = share(c, t, steps) + near_in[c, t, n].astype(jnp.float32)
            far_out[c, t, n] = total.astype(jnp.bfloat16)
            far_copy(c, t, n).start()

    def finish(c, t):
        near_copy(c, t, 2).wait_recv()
        total = share(c, t, 0) + near_in[c, t, 3].astype(jnp.float32)
        for n in (1, 2, 0):
            far_copy(c, t, n).wait_recv()
            total += far_in[c, t, n].astype(jnp.float32)
        turned = swap_halves(total)
        at = c * HALF
        rows = slice(t * BAND, (t + 1) * BAND)
        if c % 2 == 0:
            out[0, 0, rows, at : at + HALF] = total[:, :HALF]
            out[0, 1, rows, at : at + HALF] = turned[:, :HALF]
        else:
            out[0, 0, rows, at : at + HALF] = turned[:, HALF:]
            out[0, 1, rows, at : at + HALF] = total[:, HALF:]

    for c in range(CHUNKS):
        for k in range(PEERS):
            tile_copy(c, k).wait_recv()
        ready = BANDS // 2 if c == CHUNKS - 1 else BANDS
        for t in range(ready):
            fields(c, t)
        for t in range(BANDS):
            if c:
                to_far(c - 1, t)
        for t in range(BANDS):
            to_near(c, t)
            if ready + t < BANDS:
                fields(c, ready + t)
        for t in range(BANDS):
            if c > 1:
                finish(c - 2, t)
    for t in range(BANDS):
        to_far(CHUNKS - 1, t)
    for t in range(BANDS):
        finish(CHUNKS - 2, t)
    for t in range(BANDS):
        finish(CHUNKS - 1, t)

    for c in range(CHUNKS):
        for k in range(PEERS):
            tile_copy(c, k).wait_send()
        for t in range(BANDS):
            pair_copy(c, t).wait_send()
            for n in range(3):
                near_copy(c, t, n).wait_send()
                far_copy(c, t, n).wait_send()
    for k in range(PEERS):
        head_copy(k).wait_send()


def on_device(kernel_v, kernel_u, sources, ranks, row_owner):
    count = 2 * NZ
    phase = (np.arange(1, count + 1)[None, :] * np.arange(count)[:, None]) % (2 * count)
    angle = np.float32(np.pi) * phase.astype(np.float32) / np.float32(count)
    scale = np.float32(count ** (-0.5))
    table = np.concatenate([(np.cos(angle) * scale).reshape(-1), (np.sin(angle) * scale).reshape(-1)])

    bf16, f32 = jnp.bfloat16, jnp.float32
    vmem, dma = pltpu.VMEM, pltpu.SemaphoreType.DMA
    scalars = pl.BlockSpec(memory_space=pltpu.SMEM)
    away = pl.BlockSpec(memory_space=pl.ANY)
    rows, cols, parts, slots, tile = kernel_v.shape[1:]
    return pl.pallas_call(
        kernel,
        out_shape=jax.ShapeDtypeStruct((1, OWN, TILE, WIDTH), f32),
        in_specs=[scalars, scalars, scalars, away, away, away],
        out_specs=pl.BlockSpec(memory_space=pltpu.VMEM),
        scratch_shapes=[
            pltpu.SMEM((ROWS,), jnp.int32),
            vmem((GROUPS, 8, COLS * SLOTS), f32),
            vmem((cols, rows, parts, slots, tile), bf16),
            vmem(kernel_u.shape[1:], bf16),
            vmem(sources.shape[1:], bf16),
            vmem((COLS, 2, TILE, 2 * LANES), bf16),
            vmem((ROWS, COLS * SLOTS, 2 * LANES), bf16),
            vmem((CHUNKS, PEERS, PACK, LANES), bf16),
            vmem((CHUNKS, DEPTH, LANES), bf16),
            vmem((8 * GROUPS, COLS * SLOTS), f32),
            vmem((BANDS, 2 * OWN * BAND, DEPTH), bf16),
            vmem((2 * OWN * BAND, LANES), f32),
            vmem((CHUNKS, BANDS, 2, BAND, LANES), f32),
            vmem((CHUNKS, BANDS, 2, BAND, LANES), f32),
            vmem((CHUNKS, BANDS, 4, BAND, LANES), bf16),
            vmem((CHUNKS, BANDS, 4, BAND, LANES), bf16),
            vmem((CHUNKS, BANDS, 3, BAND, LANES), bf16),
            vmem((CHUNKS, BANDS, 3, BAND, LANES), bf16),
            dma((2 + COLS,)),
            dma((PEERS,)),
            dma((PEERS,)),
            dma((CHUNKS, PEERS)),
            dma((CHUNKS, PEERS)),
            dma((CHUNKS, BANDS)),
            dma((CHUNKS, BANDS)),
            dma((CHUNKS, BANDS, 3)),
            dma((CHUNKS, BANDS, 3)),
            dma((CHUNKS, BANDS, 3)),
            dma((CHUNKS, BANDS, 3)),
        ],
        compiler_params=pltpu.CompilerParams(
            collective_id=0, has_side_effects=True, vmem_limit_bytes=56 * 1024 * 1024
        ),
        cost_estimate=pl.CostEstimate(flops=6 * 10**9, bytes_accessed=10 * 2**20, transcendentals=0),
    )(row_owner, jnp.transpose(ranks[0]), table, kernel_v, kernel_u, sources)


def solution(mesh):
    return jax.shard_map(
        on_device,
        mesh=mesh,
        in_specs=(
            P("freq", None, "tcol", None, None, None),
            P("freq", "tcol", None, None, None, None),
            P("freq", None, "tcol", None),
            P("freq", None, "tcol"),
            P(),
        ),
        out_specs=P("freq", "tcol", None, None),
        check_vma=False,
    )
```
